512 devices in a mesh: group: 16 (over y, z_lo), dev: 32 (over z_hi, x, core).
Axes of the slice: x: 4, y: 8, z: 8 (z_hi: 4, z_lo: 2; z = z_hi * 2 + z_lo), core: 2. Of those that a mesh axis runs over, the one named last changes fastest.
Arguments:
- slab: float32 [48, 4194304], P(None, ('group', 'dev'))
- flips: int32 [4194304], P(('group', 'dev')), may hold values 0 or 1
- sampled: int32 [12288], replicated, may hold values from 0 to 4194303, as said below
Outputs:
- mixed: float32 [48, 4194304], P(None, ('group', 'dev'))
- gram: float32 [48, 48], replicated
- factor: float32 [48, 48], replicated
The draws below stay inside these ranges and needn't reach their ends.
Inputs may be any that keep to these rules, and one draw needn't show every extreme that they name: `sampled`: the indices are distinct and strictly increasing.
All inputs are finite; a program needn't handle non-finite values. No bound on the sum of `flips` on one device may be relied on, other than what follows from the above.
Results may differ from the reference program's by a relative error of at most 0.000098.
Values sent between devices are 32-bit elements; how exact they have to be, the bound alone decides.
No kernel may reach another device: no remote copies, remote signals or barrier semaphores. Data moves between devices by JAX's collectives and lax.ppermute only.
A program may use at most 64 MiB of HBM per device.

```python
import jax
import jax.numpy as jnp
from jax import lax

COLS = 48
SAMPLES = 12288
NROWS = 4194304


def draw_slab(key, part):
    key = jax.random.fold_in(key, 1)
    return jnp.clip(jax.random.normal(key, (COLS, NROWS), jnp.float32), -6.0, 6.0)


def draw_sampled(key, part):
    key = jax.random.fold_in(key, 2)
    order = jax.random.permutation(key, NROWS)[:SAMPLES]
    return jnp.sort(order).astype(jnp.int32)


def plant(array, rng, least, high):
    longest = array.shape.index(max(array.shape))
    spots = []
    for shift in (0, 1):
        where = [jax.random.randint(jax.random.fold_in(rng, axis), (), 0, length) for axis, length in enumerate(array.shape)]
        where[longest] = (where[longest] + shift) % array.shape[longest]
        spots.append(tuple(where))
    return array.at[spots[0]].set(least).at[spots[1]].set(high)


def setup_inputs(seed: int = 0) -> dict:
    key_list = jax.random.split(jax.random.key(seed), 4)
    return {
        "slab": draw_slab(jax.random.fold_in(key_list[3], 71), 0),
        "flips": plant((jax.random.randint(key_list[1], (NROWS,), 0, 2) < 1).astype(jnp.int32), jax.random.fold_in(key_list[1], 1), 0, 1),
        "sampled": draw_sampled(jax.random.fold_in(key_list[3], 71), 0),
    }


def transform_block(block):
    width = block.shape[0]
    total = block.shape[1]
    field = block
    span = 1
    while span < total:
        pairs = field.reshape(width, total // (2 * span), 2, span)
        first = pairs[:, :, 0, :]
        second = pairs[:, :, 1, :]
        field = jnp.stack([first + second, first - second], axis=2).reshape(width, total)
        span = span * 2
    return field

def reference(slab, flips, sampled):
    signed = slab * (1 - 2 * flips).astype(jnp.float32)[None, :]
    grouped = signed.reshape(COLS // 8, 8, NROWS)
    mixed = lax.map(transform_block, grouped).reshape(COLS, NROWS)
    mixed = mixed * jnp.float32(1.0 / NROWS ** 0.5)
    picked = jnp.take(mixed, sampled, axis=1)
    gram = jnp.dot(picked, picked.T, precision=lax.Precision.HIGHEST) / jnp.float32(SAMPLES)
    factor = jnp.linalg.cholesky(gram).T
    return (mixed, gram, factor)
```

```python
import math

import jax
import jax.numpy as jnp
import numpy as np
from jax import lax
from jax.experimental import pallas as pl
from jax.experimental.pallas import tpu as pltpu
from jax.sharding import PartitionSpec as P

SAMPLES = 12288
AXES = ("group", "dev")
LANES = 128
A_LO = 16
VMEM = pl.BlockSpec(memory_space=pltpu.VMEM)
SMEM = pl.BlockSpec(memory_space=pltpu.SMEM)


def walsh(length):
    index = np.arange(length)
    anded = index[:, None] & index[None, :]
    parity = np.zeros((length, length), np.int32)
    for bit in range(length.bit_length() - 1):
        parity ^= anded >> bit & 1
    return (1 - 2 * parity).astype(jnp.bfloat16)


def split3(x):
    hi = x.astype(jnp.bfloat16)
    rest = x - hi.astype(jnp.float32)
    mid = rest.astype(jnp.bfloat16)
    lo = (rest - mid.astype(jnp.float32)).astype(jnp.bfloat16)
    return hi, mid, lo


def dot_nt(x, y):
    return lax.dot_general(x, y, (((1,), (1,)), ((), ())), preferred_element_type=jnp.float32)


def dot_nn(x, y):
    return lax.dot_general(x, y, (((1,), (0,)), ((), ())), preferred_element_type=jnp.float32)


def local_kernel(scale, slab_ref, flips_ref, table_ref, out_ref, field_ref):
    width, rows = slab_ref.shape
    outer = rows // LANES
    signs = (1 - 2 * flips_ref[...]).astype(jnp.float32) * scale
    for tile in range(0, width, 8):
        rows8 = pl.ds(tile, 8)
        for first in range(outer // 8):
            parts = []
            for k in range(8):
                a = k * (outer // 8) + first
                parts.append(slab_ref[rows8, pl.ds(a * LANES, LANES)] * signs[a : a + 1, :])
            for half in (4, 2, 1):
                parts = butterfly(parts, half)
            for k in range(8):
                a = k * (outer // 8) + first
                field_ref[rows8, pl.ds(a * LANES, LANES)] = parts[k]
        for first in range(0, outer, 8):
            parts = [field_ref[rows8, pl.ds((first + k) * LANES, LANES)] for k in range(8)]
            for half in (4, 2, 1):
                parts = butterfly(parts, half)
            for k in range(8):
                field_ref[rows8, pl.ds((first + k) * LANES, LANES)] = parts[k]
    table = table_ref[...]
    per = width * A_LO // LANES
    for a_hi in range(outer // A_LO):
        block = jnp.concatenate(
            [field_ref[:, pl.ds((a_hi * A_LO + a) * LANES, LANES)] for a in range(A_LO)], axis=0
        )
        hi, mid, lo = split3(block)
        turned = dot_nt(table, jnp.concatenate([hi, mid], axis=1)) + dot_nt(table[:, :LANES], lo)
        for j in range(per):
            out_ref[pl.ds(a_hi * LANES * per + j, LANES, stride=per), :] = turned[:, j * LANES : (j + 1) * LANES]


def butterfly(parts, half):
    out = list(parts)
    for k in range(len(parts)):
        if not k & half:
            out[k] = parts[k] + parts[k | half]
            out[k | half] = parts[k] - parts[k | half]
    return out


def blocks_kernel(x_ref, table_ref, out_ref):
    blocks = table_ref.shape[0]
    per = x_ref.shape[0] // blocks
    table = table_ref[...]
    for j in range(0, per, 2):
        x = jnp.concatenate([x_ref[pl.ds(j + i, blocks, stride=per), :] for i in range(2)], axis=1)
        hi, mid, lo = split3(x)
        y = dot_nn(table, hi) + dot_nn(table, mid) + dot_nn(table, lo)
        for i in range(2):
            out_ref[pl.ds(j + i, blocks, stride=per), :] = y[:, i * LANES : (i + 1) * LANES]


def hits_kernel(local_bits, me_ref, sampled_ref, out_ref):
    me = me_ref[0]
    s = sampled_ref[...]
    low = s & ((1 << local_bits) - 1)
    block = s >> local_bits
    a = low >> 7
    owner = (a // A_LO) * LANES + (low & (LANES - 1))
    row = jnp.where(owner == me, (a & (A_LO - 1)) * 4 + (block >> 7), -1)
    col = block & (LANES - 1)
    total = jnp.zeros(out_ref.shape, jnp.float32)
    rows_iota = lax.broadcasted_iota(jnp.int32, out_ref.shape, 0)
    cols_iota = lax.broadcasted_iota(jnp.int32, (LANES, LANES), 0)
    for start in range(0, s.shape[0], 8):
        ones_r, ones_c = [], []
        for k in range(start, start + 8):
            ones_r.append(jnp.where(rows_iota == row[k : k + 1, :], 1.0, 0.0).astype(jnp.bfloat16))
            ones_c.append(jnp.where(cols_iota == col[k : k + 1, :], 1.0, 0.0).astype(jnp.bfloat16))
        total = total + dot_nt(jnp.concatenate(ones_r, axis=1), jnp.concatenate(ones_c, axis=1))
    out_ref[...] = total


def gram_kernel(width, blocks, y_ref, hits_ref, out_ref, turned_ref):
    per = y_ref.shape[0] // blocks
    for j in range(per):
        turned_ref[pl.ds(j * LANES, LANES), :] = y_ref[pl.ds(j, blocks, stride=per), :].T
    total = jnp.zeros((3 * width, 3 * width), jnp.float32)
    for a_lo in range(A_LO):
        stacked = []
        for k in range(blocks // LANES):
            picked = (
                turned_ref[pl.ds(a_lo * width, width), pl.ds(k * LANES, LANES)]
                * hits_ref[pl.ds(a_lo * 4 + k, 1), :]
            )
            stacked.append(jnp.concatenate(split3(picked), axis=0))
        stacked = jnp.concatenate(stacked, axis=1)
        total = total + dot_nt(stacked, stacked)
    gram = jnp.zeros((width, width), jnp.float32)
    for i, k in ((2, 0), (0, 2), (1, 1), (1, 0), (0, 1), (0, 0)):
        gram = gram + total[i * width : (i + 1) * width, k * width : (k + 1) * width]
    out_ref[...] = gram


def turn_kernel(width, z_ref, out_ref):
    per = width * A_LO // LANES
    for a_hi in range(z_ref.shape[0] // (LANES * per)):
        turned = jnp.concatenate(
            [z_ref[pl.ds(a_hi * LANES * per + j, LANES, stride=per), :].T for j in range(per)], axis=0
        )
        for a_lo in range(A_LO):
            out_ref[:, pl.ds((a_hi * A_LO + a_lo) * LANES, LANES)] = turned[a_lo * width : (a_lo + 1) * width, :]


def call(kernel, shape, *operands, specs=None, scratch=(), name=None):
    return pl.pallas_call(
        kernel,
        out_shape=jax.ShapeDtypeStruct(shape, jnp.float32),
        in_specs=specs or [VMEM] * len(operands),
        out_specs=VMEM,
        scratch_shapes=list(scratch),
        compiler_params=pltpu.CompilerParams(vmem_limit_bytes=48 * 1024 * 1024),
        name=name,
    )(*operands)


def exchange(x, blocks):
    shape = x.shape
    x = lax.all_to_all(x.reshape(blocks, x.size // blocks), AXES, 0, 0, tiled=True)
    return x.reshape(shape)


def everywhere(x, axis):
    count = lax.axis_size(axis)
    x = jnp.broadcast_to(x[None], (count,) + x.shape)
    return jnp.sum(lax.all_to_all(x, axis, 0, 0, tiled=True), axis=0)


def per_device(slab, flips, sampled):
    width, rows = slab.shape
    blocks = lax.axis_size("group") * lax.axis_size("dev")
    scale = 1.0 / math.sqrt(rows * blocks)
    me = lax.axis_index(AXES).astype(jnp.int32).reshape(1)
    lines = width * rows // LANES

    table = walsh(LANES)
    local = call(
        lambda *refs: local_kernel(scale, *refs),
        (lines, LANES),
        slab,
        flips.reshape(rows // LANES, LANES),
        jnp.asarray(np.concatenate([table, table], axis=1)),
        scratch=[pltpu.VMEM((width, rows), jnp.float32)],
        name="local_transform",
    )
    there = exchange(local, blocks)
    hits = call(
        lambda *refs: hits_kernel(rows.bit_length() - 1, *refs),
        (A_LO * blocks // LANES, LANES),
        me,
        sampled.reshape(SAMPLES // LANES, LANES),
        specs=[SMEM, VMEM],
        name="sampled_hits",
    )
    whole = call(blocks_kernel, (lines, LANES), there, jnp.asarray(walsh(blocks)), name="block_transform")
    back = exchange(whole, blocks)
    mixed = call(lambda *refs: turn_kernel(width, *refs), (width, rows), back, name="turn_back")

    partial = call(
        lambda *refs: gram_kernel(width, blocks, *refs),
        (width, width),
        whole,
        hits,
        scratch=[pltpu.VMEM((width * A_LO, blocks), jnp.float32)],
        name="gram_terms",
    )
    total = everywhere(everywhere(partial, "group"), "dev")
    gram = total / jnp.float32(SAMPLES)
    factor = jnp.linalg.cholesky(gram).T
    return (mixed, gram, factor)


def solution(mesh):
    placed = (P(None, AXES), P(AXES), P())
    return jax.shard_map(
        per_device,
        mesh=mesh,
        in_specs=placed,
        out_specs=(P(None, AXES), P(), P()),
        check_vma=False,
    )
```

```python
import math

import jax
import jax.numpy as jnp
import numpy as np
from jax import lax
from jax.experimental import pallas as pl
from jax.experimental.pallas import tpu as pltpu
from jax.sharding import PartitionSpec as P

SAMPLES = 12288
AXES = ("group", "dev")
LANES = 128
A_LO = 16
PACK = 16
PIVOTS = 4
VMEM = pl.BlockSpec(memory_space=pltpu.VMEM)
HBM = pl.BlockSpec(memory_space=pltpu.HBM)
SMEM = pl.BlockSpec(memory_space=pltpu.SMEM)


def walsh(length):
    index = np.arange(length)
    anded = index[:, None] & index[None, :]
    parity = np.zeros((length, length), np.int32)
    for bit in range(length.bit_length() - 1):
        parity ^= anded >> bit & 1
    return (1 - 2 * parity).astype(jnp.bfloat16)


def split3(x):
    hi = x.astype(jnp.bfloat16)
    rest = x - hi.astype(jnp.float32)
    mid = rest.astype(jnp.bfloat16)
    lo = (rest - mid.astype(jnp.float32)).astype(jnp.bfloat16)
    return hi, mid, lo


def dot_nt(x, y):
    return lax.dot_general(x, y, (((1,), (1,)), ((), ())), preferred_element_type=jnp.float32)


def dot_nn(x, y):
    return lax.dot_general(x, y, (((1,), (0,)), ((), ())), preferred_element_type=jnp.float32)


def walsh_in_kernel(shape):
    anded = lax.broadcasted_iota(jnp.int32, shape, 0) & lax.broadcasted_iota(jnp.int32, shape, 1)
    for shift in (4, 2, 1):
        anded = anded ^ anded >> shift
    return (1 - 2 * (anded & 1)).astype(jnp.float32).astype(jnp.bfloat16)


def local_kernel(scale, slab_ref, flips_ref, out_ref, field_ref, signs_ref, turned_ref, in_sem, flip_sem, out_sem):
    width, rows = slab_ref.shape
    outer = rows // LANES
    flips_in = pltpu.make_async_copy(flips_ref, signs_ref, flip_sem)
    flips_in.start()
    slab_in = []
    for tile in range(width // 8):
        part = pl.ds(tile * 8, 8)
        slab_in.append(pltpu.make_async_copy(slab_ref.at[part], field_ref.at[part], in_sem.at[tile]))
        slab_in[-1].start()
    table = walsh_in_kernel((LANES, LANES))
    table2 = jnp.concatenate([table, table], axis=1)
    flips_in.wait()
    signs = (1 - 2 * signs_ref[...]).astype(jnp.float32) * scale
    for tile in range(width // 8):
        rows8 = pl.ds(tile * 8, 8)
        slab_in[tile].wait()
        for first in range(outer // 8):
            parts = []
            for k in range(8):
                a = k * (outer // 8) + first
                parts.append(field_ref[rows8, pl.ds(a * LANES, LANES)] * signs[a : a + 1, :])
            for half in (4, 2, 1):
                parts = butterfly(parts, half)
            for k in range(8):
                a = k * (outer // 8) + first
                field_ref[rows8, pl.ds(a * LANES, LANES)] = parts[k]
        for first in range(0, outer, 8):
            parts = [field_ref[rows8, pl.ds((first + k) * LANES, LANES)] for k in range(8)]
            for half in (4, 2, 1):
                parts = butterfly(parts, half)
            for k in range(8):
                field_ref[rows8, pl.ds((first + k) * LANES, LANES)] = parts[k]
    per = width * A_LO // LANES
    out = []
    for a_hi in range(outer // A_LO):
        block = jnp.concatenate(
            [field_ref[:, pl.ds((a_hi * A_LO + a) * LANES, LANES)] for a in range(A_LO)], axis=0
        )
        hi, mid, lo = split3(block)
        turned = dot_nt(table2, jnp.concatenate([hi, mid], axis=1)) + dot_nt(table, lo)
        for j in range(per):
            turned_ref[pl.ds(a_hi * LANES * per + j, LANES, stride=per), :] = turned[:, j * LANES : (j + 1) * LANES]
        part = pl.ds(a_hi * LANES * per, LANES * per)
        out.append(pltpu.make_async_copy(turned_ref.at[part], out_ref.at[part], out_sem.at[a_hi]))
        out[-1].start()
    for copy in out:
        copy.wait()


def butterfly(parts, half):
    out = list(parts)
    for k in range(len(parts)):
        if not k & half:
            out[k] = parts[k] + parts[k | half]
            out[k | half] = parts[k] - parts[k | half]
    return out


def blocks_kernel(width, x_ref, table_ref, hits_ref, out_ref, packed_ref, y_ref, turned_ref, out_sem):
    blocks = table_ref.shape[0]
    per = x_ref.shape[0] // blocks
    table = table_ref[...]
    for j in range(0, per, 2):
        x = jnp.concatenate([x_ref[pl.ds(j + i, blocks, stride=per), :] for i in range(2)], axis=1)
        hi, mid, lo = split3(x)
        y = dot_nn(table, hi) + dot_nn(table, mid) + dot_nn(table, lo)
        for i in range(2):
            part = y[:, i * LANES : (i + 1) * LANES]
            y_ref[pl.ds(j + i, blocks, stride=per), :] = part
            turned_ref[pl.ds((j + i) * LANES, LANES), :] = part.T
    out = pltpu.make_async_copy(y_ref, out_ref, out_sem)
    out.start()
    gram_terms(width, turned_ref, hits_ref, packed_ref)
    out.wait()


def hits_kernel(local_bits, me_ref, sampled_ref, out_ref):
    me = me_ref[0]
    s = sampled_ref[...]
    low = s & ((1 << local_bits) - 1)
    block = s >> local_bits
    a = low >> 7
    owner = (a // A_LO) * LANES + (low & (LANES - 1))
    row = jnp.where(owner == me, (a & (A_LO - 1)) * 4 + (block >> 7), -1)
    col = block & (LANES - 1)
    total = jnp.zeros(out_ref.shape, jnp.float32)
    rows_iota = lax.broadcasted_iota(jnp.int32, out_ref.shape, 0)
    cols_iota = lax.broadcasted_iota(jnp.int32, (LANES, LANES), 0)
    for start in range(0, s.shape[0], 8):
        ones_r, ones_c = [], []
        for k in range(start, start + 8):
            ones_r.append(jnp.where(rows_iota == row[k : k + 1, :], 1.0, 0.0).astype(jnp.bfloat16))
            ones_c.append(jnp.where(cols_iota == col[k : k + 1, :], 1.0, 0.0).astype(jnp.bfloat16))
        total = total + dot_nt(jnp.concatenate(ones_r, axis=1), jnp.concatenate(ones_c, axis=1))
    out_ref[...] = total


def gram_terms(width, turned_ref, hits_ref, out_ref):
    blocks = turned_ref.shape[1]
    total = jnp.zeros((3 * width, 3 * width), jnp.float32)
    for a_lo in range(A_LO):
        stacked = []
        for k in range(blocks // LANES):
            picked = (
                turned_ref[pl.ds(a_lo * width, width), pl.ds(k * LANES, LANES)]
                * hits_ref[pl.ds(a_lo * 4 + k, 1), :]
            )
            stacked.append(jnp.concatenate(split3(picked), axis=0))
        stacked = jnp.concatenate(stacked, axis=1)
        total = total + dot_nt(stacked, stacked)
    gram = jnp.zeros((width, width), jnp.float32)
    for i, k in ((2, 0), (0, 2), (1, 1), (1, 0), (0, 1), (0, 0)):
        gram = gram + total[i * width : (i + 1) * width, k * width : (k + 1) * width]
    out_ref[...] = jnp.zeros_like(out_ref)
    at = 0
    for i in range(0, width, PACK):
        out_ref[:, pl.ds(at, width - i)] = gram[i : i + PACK, i:]
        at += width - i


def factor_kernel(x_ref, partner_ref, gram_ref, factor_ref, full_ref):
    width = gram_ref.shape[0]
    packed = (x_ref[...] + partner_ref[...]) / jnp.float32(SAMPLES)
    full_ref[...] = jnp.zeros_like(full_ref)
    at = 0
    for i in range(0, width, PACK):
        full_ref[pl.ds(i, PACK), pl.ds(i, width - i)] = packed[:, at : at + width - i]
        at += width - i
    for i in range(0, width, PACK):
        for k in range(i + PACK, width, PACK):
            full_ref[pl.ds(k, PACK), pl.ds(i, PACK)] = full_ref[pl.ds(i, PACK), pl.ds(k, PACK)].T
    left = full_ref[...]
    gram_ref[...] = left[:, :width]
    lane = lax.broadcasted_iota(jnp.int32, (1, LANES), 1)
    upper = []
    for at in range(0, width, PIVOTS):
        rows = [left[at + i : at + i + 1, :] for i in range(PIVOTS)]
        cols = [jnp.broadcast_to(left[:, at + i : at + i + 1], left.shape) for i in range(PIVOTS)]
        pivot = [
            [jnp.broadcast_to(rows[i][:, at + k : at + k + 1], (1, LANES)) for k in range(PIVOTS)]
            for i in range(PIVOTS)
        ]
        for i in range(PIVOTS):
            inverse = 1.0 / pivot[i][i]
            for k in range(i + 1, PIVOTS):
                ratio = pivot[i][k] * inverse
                rows[k] = rows[k] - ratio * rows[i]
                cols[k] = cols[k] - ratio * cols[i]
                for m in range(k, PIVOTS):
                    pivot[k][m] = pivot[k][m] - ratio * pivot[i][m]
            upper.append(jnp.where(lane >= at + i, rows[i] / jnp.sqrt(pivot[i][i]), 0.0))
            left = left - cols[i] * (rows[i] * inverse)
    for i in range(width):
        factor_ref[pl.ds(i, 1), :] = upper[i][:, :width]


def turn_kernel(width, z_ref, out_ref, turned_ref, out_sem):
    per = width * A_LO // LANES
    out = []
    for a_hi in range(z_ref.shape[0] // (LANES * per)):
        turned = jnp.concatenate(
            [z_ref[pl.ds(a_hi * LANES * per + j, LANES, stride=per), :].T for j in range(per)], axis=0
        )
        for a_lo in range(A_LO):
            turned_ref[:, pl.ds((a_hi * A_LO + a_lo) * LANES, LANES)] = turned[a_lo * width : (a_lo + 1) * width, :]
        part = (slice(None), pl.ds(a_hi * A_LO * LANES, A_LO * LANES))
        out.append(pltpu.make_async_copy(turned_ref.at[part], out_ref.at[part], out_sem.at[a_hi]))
        out[-1].start()
    for copy in out:
        copy.wait()


def call(kernel, shapes, *operands, specs=None, out_specs=None, scratch=(), name=None):
    out = [jax.ShapeDtypeStruct(shape, jnp.float32) for shape in shapes]
    return pl.pallas_call(
        kernel,
        out_shape=out,
        in_specs=specs or [VMEM] * len(operands),
        out_specs=out_specs or [VMEM] * len(out),
        scratch_shapes=list(scratch),
        compiler_params=pltpu.CompilerParams(vmem_limit_bytes=48 * 1024 * 1024),
        name=name,
    )(*operands)


def exchange(x, blocks):
    shape = x.shape
    x = lax.all_to_all(x.reshape(blocks, x.size // blocks), AXES, 0, 0, tiled=True)
    return x.reshape(shape)


def sum_over(x, axis):
    count = lax.axis_size(axis)
    x = jnp.broadcast_to(x[None], (count,) + x.shape)
    return jnp.sum(lax.all_to_all(x, axis, 0, 0, tiled=True), axis=0)


def sum_pairwise(x, axis):
    count = lax.axis_size(axis)
    partner = jnp.zeros_like(x)
    for bit in range(count.bit_length() - 1):
        x = x + partner if bit else x
        partner = lax.ppermute(x, axis, [(i, i ^ 1 << bit) for i in range(count)])
    return x, partner


def per_device(slab, flips, sampled):
    width, rows = slab.shape
    blocks = lax.axis_size("group") * lax.axis_size("dev")
    scale = 1.0 / math.sqrt(rows * blocks)
    me = lax.axis_index(AXES).astype(jnp.int32).reshape(1)
    lines = width * rows // LANES
    outer = rows // LANES
    dma = pltpu.SemaphoreType.DMA

    (local,) = call(
        lambda *refs: local_kernel(scale, *refs),
        [(lines, LANES)],
        slab,
        flips.reshape(outer, LANES),
        specs=[HBM, HBM],
        out_specs=[HBM],
        scratch=[
            pltpu.VMEM((width, rows), jnp.float32),
            pltpu.VMEM((outer, LANES), jnp.int32),
            pltpu.VMEM((lines, LANES), jnp.float32),
            dma((width // 8,)),
            dma,
            dma((outer // A_LO,)),
        ],
        name="local_transform",
    )
    there = exchange(local, blocks)
    (hits,) = call(
        lambda *refs: hits_kernel(rows.bit_length() - 1, *refs),
        [(A_LO * blocks // LANES, LANES)],
        me,
        sampled.reshape(SAMPLES // LANES, LANES),
        specs=[SMEM, VMEM],
        name="sampled_hits",
    )
    whole, partial = call(
        lambda *refs: blocks_kernel(width, *refs),
        [(lines, LANES), (PACK, LANES)],
        there,
        jnp.asarray(walsh(blocks)),
        hits,
        out_specs=[HBM, VMEM],
        scratch=[pltpu.VMEM((lines, LANES), jnp.float32), pltpu.VMEM((width * A_LO, blocks), jnp.float32), dma],
        name="block_transform",
    )
    whole, partial = lax.optimization_barrier((whole, sum_over(partial, "group")))
    back = exchange(whole, blocks)
    (mixed,) = call(
        lambda *refs: turn_kernel(width, *refs),
        [(width, rows)],
        back,
        out_specs=[HBM],
        scratch=[pltpu.VMEM((width, rows), jnp.float32), dma((outer // A_LO,))],
        name="turn_back",
    )
    gram, factor = call(
        factor_kernel,
        [(width, width)] * 2,
        *sum_pairwise(partial, "dev"),
        scratch=[pltpu.VMEM((width, LANES), jnp.float32)],
        name="factor",
    )
    return (mixed, gram, factor)


def solution(mesh):
    placed = (P(None, AXES), P(AXES), P())
    return jax.shard_map(
        per_device,
        mesh=mesh,
        in_specs=placed,
        out_specs=(P(None, AXES), P(), P()),
        check_vma=False,
    )
```

```python
import math

import jax
import jax.numpy as jnp
import numpy as np
from jax import lax
from jax.experimental import pallas as pl
from jax.experimental.pallas import tpu as pltpu
from jax.sharding import PartitionSpec as P

SAMPLES = 12288
AXES = ("group", "dev")
LANES = 128
A_LO = 16
PACK = 16
FAR = (5, 6, 7, 8)
NEAR = (0,)
MIDDLE = (1, 2)
LAST = (3, 4)
PIVOTS = 8
VMEM = pl.BlockSpec(memory_space=pltpu.VMEM)
HBM = pl.BlockSpec(memory_space=pltpu.HBM)
SMEM = pl.BlockSpec(memory_space=pltpu.SMEM)


def walsh(length):
    index = np.arange(length)
    anded = index[:, None] & index[None, :]
    parity = np.zeros((length, length), np.int32)
    for bit in range(length.bit_length() - 1):
        parity ^= anded >> bit & 1
    return (1 - 2 * parity).astype(jnp.bfloat16)


def split3(x):
    hi = x.astype(jnp.bfloat16)
    rest = x - hi.astype(jnp.float32)
    mid = rest.astype(jnp.bfloat16)
    lo = (rest - mid.astype(jnp.float32)).astype(jnp.bfloat16)
    return hi, mid, lo


def dot_nt(x, y):
    return lax.dot_general(x, y, (((1,), (1,)), ((), ())), preferred_element_type=jnp.float32)


def dot_nn(x, y):
    return lax.dot_general(x, y, (((1,), (0,)), ((), ())), preferred_element_type=jnp.float32)


def walsh_in_kernel(shape):
    anded = lax.broadcasted_iota(jnp.int32, shape, 0) & lax.broadcasted_iota(jnp.int32, shape, 1)
    for shift in (4, 2, 1):
        anded = anded ^ anded >> shift
    return (1 - 2 * (anded & 1)).astype(jnp.float32).astype(jnp.bfloat16)


def local_kernel(scale, slab_ref, flips_ref, out_ref, field_ref, signs_ref, turned_ref, in_sem, flip_sem, out_sem):
    width, rows = slab_ref.shape
    outer = rows // LANES
    flips_in = pltpu.make_async_copy(flips_ref, signs_ref, flip_sem)
    flips_in.start()
    slab_in = []
    for tile in range(width // 8):
        part = pl.ds(tile * 8, 8)
        slab_in.append(pltpu.make_async_copy(slab_ref.at[part], field_ref.at[part], in_sem.at[tile]))
        slab_in[-1].start()
    table = walsh_in_kernel((LANES, LANES))
    table2 = jnp.concatenate([table, table], axis=1)
    flips_in.wait()
    signs = (1 - 2 * signs_ref[...]).astype(jnp.float32) * scale
    for tile in range(width // 8):
        rows8 = pl.ds(tile * 8, 8)
        slab_in[tile].wait()
        for first in range(outer // 8):
            parts = []
            for k in range(8):
                a = k * (outer // 8) + first
                parts.append(field_ref[rows8, pl.ds(a * LANES, LANES)] * signs[a : a + 1, :])
            for half in (4, 2, 1):
                parts = butterfly(parts, half)
            for k in range(8):
                a = k * (outer // 8) + first
                field_ref[rows8, pl.ds(a * LANES, LANES)] = parts[k]
        for first in range(0, outer, 8):
            parts = [field_ref[rows8, pl.ds((first + k) * LANES, LANES)] for k in range(8)]
            for half in (4, 2, 1):
                parts = butterfly(parts, half)
            for k in range(8):
                field_ref[rows8, pl.ds((first + k) * LANES, LANES)] = parts[k]
    per = width * A_LO // LANES
    out = []
    for a_hi in range(outer // A_LO):
        block = jnp.concatenate(
            [field_ref[:, pl.ds((a_hi * A_LO + a) * LANES, LANES)] for a in range(A_LO)], axis=0
        )
        hi, mid, lo = split3(block)
        turned = dot_nt(table2, jnp.concatenate([hi, mid], axis=1)) + dot_nt(table, lo)
        for j in range(per):
            turned_ref[pl.ds(a_hi * LANES * per + j, LANES, stride=per), :] = turned[:, j * LANES : (j + 1) * LANES]
        part = pl.ds(a_hi * LANES * per, LANES * per)
        out.append(pltpu.make_async_copy(turned_ref.at[part], out_ref.at[part], out_sem.at[a_hi]))
        out[-1].start()
    for copy in out:
        copy.wait()


def butterfly(parts, half):
    out = list(parts)
    for k in range(len(parts)):
        if not k & half:
            out[k] = parts[k] + parts[k | half]
            out[k | half] = parts[k] - parts[k | half]
    return out


def blocks_kernel(x_ref, table_ref, out_ref, y_ref, out_sem):
    blocks = table_ref.shape[0]
    per = x_ref.shape[0] // blocks
    table = table_ref[...]
    for j in range(0, per, 2):
        x = jnp.concatenate([x_ref[pl.ds(j + i, blocks, stride=per), :] for i in range(2)], axis=1)
        hi, mid, lo = split3(x)
        y = dot_nn(table, hi) + dot_nn(table, mid) + dot_nn(table, lo)
        for i in range(2):
            y_ref[pl.ds(j + i, blocks, stride=per), :] = y[:, i * LANES : (i + 1) * LANES]
    out = pltpu.make_async_copy(y_ref, out_ref, out_sem)
    out.start()
    out.wait()


def gram_kernel(width, blocks, y_ref, hits_ref, packed_ref, turned_ref):
    per = y_ref.shape[0] // blocks
    for j in range(per):
        turned_ref[pl.ds(j * LANES, LANES), :] = y_ref[pl.ds(j, blocks, stride=per), :].T
    gram_terms(width, turned_ref, hits_ref, packed_ref)


def hits_kernel(local_bits, me_ref, sampled_ref, out_ref):
    me = me_ref[0]
    s = sampled_ref[...]
    low = s & ((1 << local_bits) - 1)
    block = s >> local_bits
    a = low >> 7
    owner = (a // A_LO) * LANES + (low & (LANES - 1))
    row = jnp.where(owner == me, (a & (A_LO - 1)) * 4 + (block >> 7), -1)
    col = block & (LANES - 1)
    total = jnp.zeros(out_ref.shape, jnp.float32)
    rows_iota = lax.broadcasted_iota(jnp.int32, out_ref.shape, 0)
    cols_iota = lax.broadcasted_iota(jnp.int32, (LANES, LANES), 0)
    for start in range(0, s.shape[0], 8):
        ones_r, ones_c = [], []
        for k in range(start, start + 8):
            ones_r.append(jnp.where(rows_iota == row[k : k + 1, :], 1.0, 0.0).astype(jnp.bfloat16))
            ones_c.append(jnp.where(cols_iota == col[k : k + 1, :], 1.0, 0.0).astype(jnp.bfloat16))
        total = total + dot_nt(jnp.concatenate(ones_r, axis=1), jnp.concatenate(ones_c, axis=1))
    out_ref[...] = total


def gram_terms(width, turned_ref, hits_ref, out_ref):
    blocks = turned_ref.shape[1]
    total = jnp.zeros((3 * width, 3 * width), jnp.float32)
    for a_lo in range(A_LO):
        stacked = []
        for k in range(blocks // LANES):
            picked = (
                turned_ref[pl.ds(a_lo * width, width), pl.ds(k * LANES, LANES)]
                * hits_ref[pl.ds(a_lo * 4 + k, 1), :]
            )
            stacked.append(jnp.concatenate(split3(picked), axis=0))
        stacked = jnp.concatenate(stacked, axis=1)
        total = total + dot_nt(stacked, stacked)
    gram = jnp.zeros((width, width), jnp.float32)
    for i, k in ((2, 0), (0, 2), (1, 1), (1, 0), (0, 1), (0, 0)):
        gram = gram + total[i * width : (i + 1) * width, k * width : (k + 1) * width]
    out_ref[...] = jnp.zeros_like(out_ref)
    at = 0
    for i in range(0, width, PACK):
        out_ref[:, pl.ds(at, width - i)] = gram[i : i + PACK, i:]
        at += width - i


def copies_kernel(x_ref, one_ref, two_ref, three_ref, out_ref):
    total = (x_ref[...] + one_ref[...]) + (two_ref[...] + three_ref[...])
    for k in range(out_ref.shape[0]):
        out_ref[k] = total


def factor_kernel(x_ref, gram_ref, factor_ref, full_ref):
    width = gram_ref.shape[0]
    packed = x_ref[...] / jnp.float32(SAMPLES)
    full_ref[...] = jnp.zeros_like(full_ref)
    at = 0
    for i in range(0, width, PACK):
        full_ref[pl.ds(i, PACK), pl.ds(i, width - i)] = packed[:, at : at + width - i]
        at += width - i
    for i in range(0, width, PACK):
        for k in range(i + PACK, width, PACK):
            full_ref[pl.ds(k, PACK), pl.ds(i, PACK)] = full_ref[pl.ds(i, PACK), pl.ds(k, PACK)].T
    left = full_ref[...]
    gram_ref[...] = left[:, :width]
    lane = lax.broadcasted_iota(jnp.int32, (1, LANES), 1)
    upper = []
    for at in range(0, width, PIVOTS):
        rows = [left[at + i : at + i + 1, :] for i in range(PIVOTS)]
        cols = [jnp.broadcast_to(left[:, at + i : at + i + 1], left.shape) for i in range(PIVOTS)]
        pivot = [
            [jnp.broadcast_to(rows[i][:, at + k : at + k + 1], (1, LANES)) for k in range(PIVOTS)]
            for i in range(PIVOTS)
        ]
        for i in range(PIVOTS):
            inverse = 1.0 / pivot[i][i]
            for k in range(i + 1, PIVOTS):
                ratio = pivot[i][k] * inverse
                rows[k] = rows[k] - ratio * rows[i]
                cols[k] = cols[k] - ratio * cols[i]
                for m in range(k, PIVOTS):
                    pivot[k][m] = pivot[k][m] - ratio * pivot[i][m]
            upper.append(jnp.where(lane >= at + i, rows[i] / jnp.sqrt(pivot[i][i]), 0.0))
            left = left - cols[i] * (rows[i] * inverse)
    for i in range(width):
        factor_ref[pl.ds(i, 1), :] = upper[i][:, :width]


def turn_kernel(width, z_ref, out_ref, turned_ref, out_sem):
    per = width * A_LO // LANES
    out = []
    for a_hi in range(z_ref.shape[0] // (LANES * per)):
        turned = jnp.concatenate(
            [z_ref[pl.ds(a_hi * LANES * per + j, LANES, stride=per), :].T for j in range(per)], axis=0
        )
        for a_lo in range(A_LO):
            turned_ref[:, pl.ds((a_hi * A_LO + a_lo) * LANES, LANES)] = turned[a_lo * width : (a_lo + 1) * width, :]
        part = (slice(None), pl.ds(a_hi * A_LO * LANES, A_LO * LANES))
        out.append(pltpu.make_async_copy(turned_ref.at[part], out_ref.at[part], out_sem.at[a_hi]))
        out[-1].start()
    for copy in out:
        copy.wait()


def call(kernel, shapes, *operands, specs=None, out_specs=None, scratch=(), name=None):
    out = [jax.ShapeDtypeStruct(shape, jnp.float32) for shape in shapes]
    return pl.pallas_call(
        kernel,
        out_shape=out,
        in_specs=specs or [VMEM] * len(operands),
        out_specs=out_specs or [VMEM] * len(out),
        scratch_shapes=list(scratch),
        compiler_params=pltpu.CompilerParams(vmem_limit_bytes=48 * 1024 * 1024),
        name=name,
    )(*operands)


def exchange(x, blocks):
    shape = x.shape
    x = lax.all_to_all(x.reshape(blocks, x.size // blocks), AXES, 0, 0, tiled=True)
    return x.reshape(shape)


def sum_over(x, bits):
    total = lax.axis_size(AXES)
    member = [sum((k >> n & 1) << bit for n, bit in enumerate(bits)) for k in range(1 << len(bits))]
    groups = [[i | m for m in member] for i in range(total) if not i & member[-1]]
    return jnp.sum(lax.all_to_all(x, AXES, 0, 0, tiled=True, axis_index_groups=groups), axis=0)


def sum_pairwise(x, bits):
    for bit in bits:
        x = x + from_partner(x, 1 << bit)
    return x


def from_others(x, bits):
    return [from_partner(x, apart) for apart in (1 << bits[0], 1 << bits[1], 1 << bits[0] | 1 << bits[1])]


def from_partner(x, apart):
    return lax.ppermute(x, AXES, [(i, i ^ apart) for i in range(lax.axis_size(AXES))])


def per_device(slab, flips, sampled):
    width, rows = slab.shape
    blocks = lax.axis_size("group") * lax.axis_size("dev")
    scale = 1.0 / math.sqrt(rows * blocks)
    me = lax.axis_index(AXES).astype(jnp.int32).reshape(1)
    lines = width * rows // LANES
    outer = rows // LANES
    dma = pltpu.SemaphoreType.DMA

    (local,) = call(
        lambda *refs: local_kernel(scale, *refs),
        [(lines, LANES)],
        pltpu.with_memory_space_constraint(slab, pltpu.HBM),
        pltpu.with_memory_space_constraint(flips.reshape(outer, LANES), pltpu.HBM),
        specs=[HBM, HBM],
        out_specs=[HBM],
        scratch=[
            pltpu.VMEM((width, rows), jnp.float32),
            pltpu.VMEM((outer, LANES), jnp.int32),
            pltpu.VMEM((lines, LANES), jnp.float32),
            dma((width // 8,)),
            dma,
            dma((outer // A_LO,)),
        ],
        name="local_transform",
    )
    there = exchange(local, blocks)
    (hits,) = call(
        lambda *refs: hits_kernel(rows.bit_length() - 1, *refs),
        [(A_LO * blocks // LANES, LANES)],
        me,
        sampled.reshape(SAMPLES // LANES, LANES),
        specs=[SMEM, VMEM],
        name="sampled_hits",
    )
    there, hits = lax.optimization_barrier((there, hits))
    (whole,) = call(
        blocks_kernel,
        [(lines, LANES)],
        there,
        jnp.asarray(walsh(blocks)),
        out_specs=[HBM],
        scratch=[pltpu.VMEM((lines, LANES), jnp.float32), dma],
        name="block_transform",
    )
    back = exchange(whole, blocks)
    (partial,) = call(
        lambda *refs: gram_kernel(width, blocks, *refs),
        [(PACK, LANES)],
        whole,
        hits,
        scratch=[pltpu.VMEM((width * A_LO, blocks), jnp.float32)],
        name="gram_terms",
    )
    partial = sum_pairwise(partial, NEAR)
    one, two, three = from_others(partial, MIDDLE)
    partial = (partial + one) + (two + three)
    (partial,) = call(
        copies_kernel,
        [(1 << len(FAR), PACK, LANES)],
        partial,
        *from_others(partial, LAST),
        name="gram_copies",
    )
    back, partial = lax.optimization_barrier((back, partial))
    total = sum_over(partial, FAR)
    (mixed,) = call(
        lambda *refs: turn_kernel(width, *refs),
        [(width, rows)],
        back,
        out_specs=[HBM],
        scratch=[pltpu.VMEM((width, rows), jnp.float32), dma((outer // A_LO,))],
        name="turn_back",
    )
    gram, factor = call(
        factor_kernel,
        [(width, width)] * 2,
        total,
        scratch=[pltpu.VMEM((width, LANES), jnp.float32)],
        name="factor",
    )
    return (mixed, gram, factor)


def solution(mesh):
    placed = (P(None, AXES), P(AXES), P())
    return jax.shard_map(
        per_device,
        mesh=mesh,
        in_specs=placed,
        out_specs=(P(None, AXES), P(), P()),
        check_vma=False,
    )
```

```python
import math

import jax
import jax.numpy as jnp
from jax import lax
from jax.experimental import pallas as pl
from jax.experimental.pallas import tpu as pltpu
from jax.sharding import PartitionSpec as P

SAMPLES = 12288
AXES = ("group", "dev")
LANES = 128
A_LO = 16
PACK = 16
FAR = (5, 6, 7, 8)
NEAR = (0,)
MIDDLE = (1, 2)
LAST = (3, 4)
PIVOTS = 8
VMEM = pl.BlockSpec(memory_space=pltpu.VMEM)
HBM = pl.BlockSpec(memory_space=pltpu.HBM)
SMEM = pl.BlockSpec(memory_space=pltpu.SMEM)


def split3(x):
    hi = x.astype(jnp.bfloat16)
    rest = x - hi.astype(jnp.float32)
    mid = rest.astype(jnp.bfloat16)
    lo = (rest - mid.astype(jnp.float32)).astype(jnp.bfloat16)
    return hi, mid, lo


def dot_nt(x, y):
    return lax.dot_general(x, y, (((1,), (1,)), ((), ())), preferred_element_type=jnp.float32)


def local_kernel(scale, slab_ref, flips_ref, out_ref, field_ref, signs_ref, turned_ref, done_ref, in_sem, flip_sem, out_sem):
    width, rows = slab_ref.shape
    outer = rows // LANES
    flips_in = pltpu.make_async_copy(flips_ref, signs_ref, flip_sem)
    flips_in.start()
    slab_in = []
    for tile in range(width // 8):
        part = pl.ds(tile * 8, 8)
        slab_in.append(pltpu.make_async_copy(slab_ref.at[part], field_ref.at[part], in_sem.at[tile]))
        slab_in[-1].start()
    flips_in.wait()
    signs = (1 - 2 * signs_ref[...]).astype(jnp.float32) * scale
    for tile in range(width // 8):
        rows8 = pl.ds(tile * 8, 8)
        slab_in[tile].wait()
        for first in range(outer // 8):
            parts = []
            for k in range(8):
                a = k * (outer // 8) + first
                parts.append(field_ref[rows8, pl.ds(a * LANES, LANES)] * signs[a : a + 1, :])
            for half in (4, 2, 1):
                parts = butterfly(parts, half)
            for k in range(8):
                a = k * (outer // 8) + first
                field_ref[rows8, pl.ds(a * LANES, LANES)] = parts[k]
    per = width * A_LO // LANES
    out = []
    for a_hi in range(outer // A_LO):
        for first in range(a_hi * A_LO, (a_hi + 1) * A_LO, 8):
            for tile in range(width // 8):
                rows8 = pl.ds(tile * 8, 8)
                parts = [field_ref[rows8, pl.ds((first + k) * LANES, LANES)] for k in range(8)]
                for half in (4, 2, 1):
                    parts = butterfly(parts, half)
                for k in range(8):
                    field_ref[rows8, pl.ds((first + k) * LANES, LANES)] = parts[k]
        block = jnp.concatenate(
            [field_ref[:, pl.ds((a_hi * A_LO + a) * LANES, LANES)] for a in range(A_LO)], axis=0
        )
        for j in range(per):
            start = (a_hi * per + j) * LANES
            turned = block[j * LANES : (j + 1) * LANES, :].T
            parts = [turned[k : k + 8, :] for k in range(0, LANES, 8)]
            for half in (8, 4, 2, 1):
                parts = butterfly(parts, half)
            for k in range(LANES // 8):
                turned_ref[pl.ds(start + 8 * k, 8), :] = parts[k]
            parts = [turned_ref[pl.ds(start + k, LANES // 8, stride=8), :] for k in range(8)]
            for half in (4, 2, 1):
                parts = butterfly(parts, half)
            for k in range(8):
                done_ref[pl.ds((a_hi * LANES + k) * per + j, LANES // 8, stride=8 * per), :] = parts[k]
        part = pl.ds(a_hi * LANES * per, LANES * per)
        out.append(pltpu.make_async_copy(done_ref.at[part], out_ref.at[part], out_sem.at[a_hi]))
        out[-1].start()
    for copy in out:
        copy.wait()


def butterfly(parts, half):
    out = list(parts)
    for k in range(len(parts)):
        if not k & half:
            out[k] = parts[k] + parts[k | half]
            out[k | half] = parts[k] - parts[k | half]
    return out


def blocks_kernel(blocks, x_ref, out_ref, half_ref, y_ref, out_sem):
    per = x_ref.shape[0] // blocks
    far = blocks // 8
    for j in range(per):
        for first in range(0, far, 8):
            parts = [x_ref[pl.ds((k * far + first) * per + j, 8, stride=per), :] for k in range(8)]
            for half in (4, 2, 1):
                parts = butterfly(parts, half)
            for k in range(8):
                half_ref[pl.ds(j * blocks + k * far + first, 8), :] = parts[k]
    out = []
    for first in range(0, blocks, 64):
        for j in range(per):
            start = j * blocks + first
            parts = [half_ref[pl.ds(start + 8 * k, 8), :] for k in range(8)]
            for half in (4, 2, 1):
                parts = butterfly(parts, half)
            for k in range(8):
                half_ref[pl.ds(start + 8 * k, 8), :] = parts[k]
            parts = [half_ref[pl.ds(start + k, 8, stride=8), :] for k in range(8)]
            for half in (4, 2, 1):
                parts = butterfly(parts, half)
            for k in range(8):
                y_ref[pl.ds((first + k) * per + j, 8, stride=8 * per), :] = parts[k]
        part = pl.ds(first * per, 64 * per)
        out.append(pltpu.make_async_copy(y_ref.at[part], out_ref.at[part], out_sem.at[first // 64]))
        out[-1].start()
    for copy in out:
        copy.wait()


def gram_kernel(width, blocks, y_ref, hits_ref, packed_ref, turned_ref):
    per = y_ref.shape[0] // blocks
    for j in range(per):
        turned_ref[pl.ds(j * LANES, LANES), :] = y_ref[pl.ds(j, blocks, stride=per), :].T
    gram_terms(width, turned_ref, hits_ref, packed_ref)


def hits_kernel(local_bits, me_ref, sampled_ref, out_ref):
    me = me_ref[0]
    s = sampled_ref[...]
    low = s & ((1 << local_bits) - 1)
    block = s >> local_bits
    a = low >> 7
    owner = (a // A_LO) * LANES + (low & (LANES - 1))
    row = jnp.where(owner == me, (a & (A_LO - 1)) * 4 + (block >> 7), -1)
    col = block & (LANES - 1)
    total = jnp.zeros(out_ref.shape, jnp.float32)
    rows_iota = lax.broadcasted_iota(jnp.int32, out_ref.shape, 0)
    cols_iota = lax.broadcasted_iota(jnp.int32, (LANES, LANES), 0)
    for start in range(0, s.shape[0], 8):
        ones_r, ones_c = [], []
        for k in range(start, start + 8):
            ones_r.append(jnp.where(rows_iota == row[k : k + 1, :], 1.0, 0.0).astype(jnp.bfloat16))
            ones_c.append(jnp.where(cols_iota == col[k : k + 1, :], 1.0, 0.0).astype(jnp.bfloat16))
        total = total + dot_nt(jnp.concatenate(ones_r, axis=1), jnp.concatenate(ones_c, axis=1))
    out_ref[...] = total


def gram_terms(width, turned_ref, hits_ref, out_ref):
    blocks = turned_ref.shape[1]
    total = jnp.zeros((3 * width, 3 * width), jnp.float32)
    for a_lo in range(A_LO):
        stacked = []
        for k in range(blocks // LANES):
            picked = (
                turned_ref[pl.ds(a_lo * width, width), pl.ds(k * LANES, LANES)]
                * hits_ref[pl.ds(a_lo * 4 + k, 1), :]
            )
            stacked.append(jnp.concatenate(split3(picked), axis=0))
        stacked = jnp.concatenate(stacked, axis=1)
        total = total + dot_nt(stacked, stacked)
    gram = jnp.zeros((width, width), jnp.float32)
    for i, k in ((2, 0), (0, 2), (1, 1), (1, 0), (0, 1), (0, 0)):
        gram = gram + total[i * width : (i + 1) * width, k * width : (k + 1) * width]
    out_ref[...] = jnp.zeros_like(out_ref)
    at = 0
    for i in range(0, width, PACK):
        out_ref[:, pl.ds(at, width - i)] = gram[i : i + PACK, i:]
        at += width - i


def copies_kernel(x_ref, one_ref, two_ref, three_ref, out_ref):
    total = (x_ref[...] + one_ref[...]) + (two_ref[...] + three_ref[...])
    for k in range(out_ref.shape[0]):
        out_ref[k] = total


def factor_kernel(x_ref, gram_ref, factor_ref, full_ref):
    width = gram_ref.shape[0]
    packed = x_ref[...] / jnp.float32(SAMPLES)
    full_ref[...] = jnp.zeros_like(full_ref)
    at = 0
    for i in range(0, width, PACK):
        full_ref[pl.ds(i, PACK), pl.ds(i, width - i)] = packed[:, at : at + width - i]
        at += width - i
    for i in range(0, width, PACK):
        for k in range(i + PACK, width, PACK):
            full_ref[pl.ds(k, PACK), pl.ds(i, PACK)] = full_ref[pl.ds(i, PACK), pl.ds(k, PACK)].T
    left = full_ref[...]
    gram_ref[...] = left[:, :width]
    lane = lax.broadcasted_iota(jnp.int32, (1, LANES), 1)
    upper = []
    for at in range(0, width, PIVOTS):
        rows = [left[at + i : at + i + 1, :] for i in range(PIVOTS)]
        cols = [jnp.broadcast_to(left[:, at + i : at + i + 1], left.shape) for i in range(PIVOTS)]
        pivot = [
            [jnp.broadcast_to(rows[i][:, at + k : at + k + 1], (1, LANES)) for k in range(PIVOTS)]
            for i in range(PIVOTS)
        ]
        for i in range(PIVOTS):
            inverse = 1.0 / pivot[i][i]
            for k in range(i + 1, PIVOTS):
                ratio = pivot[i][k] * inverse
                rows[k] = rows[k] - ratio * rows[i]
                cols[k] = cols[k] - ratio * cols[i]
                for m in range(k, PIVOTS):
                    pivot[k][m] = pivot[k][m] - ratio * pivot[i][m]
            upper.append(jnp.where(lane >= at + i, rows[i] / jnp.sqrt(pivot[i][i]), 0.0))
            left = left - cols[i] * (rows[i] * inverse)
    for i in range(width):
        factor_ref[pl.ds(i, 1), :] = upper[i][:, :width]


def turn_kernel(width, z_ref, out_ref, turned_ref, out_sem):
    per = width * A_LO // LANES
    out = []
    for a_hi in range(z_ref.shape[0] // (LANES * per)):
        turned = jnp.concatenate(
            [z_ref[pl.ds(a_hi * LANES * per + j, LANES, stride=per), :].T for j in range(per)], axis=0
        )
        for a_lo in range(A_LO):
            turned_ref[:, pl.ds((a_hi * A_LO + a_lo) * LANES, LANES)] = turned[a_lo * width : (a_lo + 1) * width, :]
        part = (slice(None), pl.ds(a_hi * A_LO * LANES, A_LO * LANES))
        out.append(pltpu.make_async_copy(turned_ref.at[part], out_ref.at[part], out_sem.at[a_hi]))
        out[-1].start()
    for copy in out:
        copy.wait()


def call(kernel, shapes, *operands, specs=None, out_specs=None, scratch=(), name=None):
    out = [jax.ShapeDtypeStruct(shape, jnp.float32) for shape in shapes]
    return pl.pallas_call(
        kernel,
        out_shape=out,
        in_specs=specs or [VMEM] * len(operands),
        out_specs=out_specs or [VMEM] * len(out),
        scratch_shapes=list(scratch),
        compiler_params=pltpu.CompilerParams(vmem_limit_bytes=48 * 1024 * 1024),
        name=name,
    )(*operands)


def exchange(x, blocks):
    shape = x.shape
    x = lax.all_to_all(x.reshape(blocks, x.size // blocks), AXES, 0, 0, tiled=True)
    return x.reshape(shape)


def sum_over(x, bits):
    total = lax.axis_size(AXES)
    member = [sum((k >> n & 1) << bit for n, bit in enumerate(bits)) for k in range(1 << len(bits))]
    groups = [[i | m for m in member] for i in range(total) if not i & member[-1]]
    return jnp.sum(lax.all_to_all(x, AXES, 0, 0, tiled=True, axis_index_groups=groups), axis=0)


def sum_pairwise(x, bits):
    for bit in bits:
        x = x + from_partner(x, 1 << bit)
    return x


def from_others(x, bits):
    return [from_partner(x, apart) for apart in (1 << bits[0], 1 << bits[1], 1 << bits[0] | 1 << bits[1])]


def from_partner(x, apart):
    return lax.ppermute(x, AXES, [(i, i ^ apart) for i in range(lax.axis_size(AXES))])


def per_device(slab, flips, sampled):
    width, rows = slab.shape
    blocks = lax.axis_size("group") * lax.axis_size("dev")
    scale = 1.0 / math.sqrt(rows * blocks)
    me = lax.axis_index(AXES).astype(jnp.int32).reshape(1)
    lines = width * rows // LANES
    outer = rows // LANES
    dma = pltpu.SemaphoreType.DMA

    (local,) = call(
        lambda *refs: local_kernel(scale, *refs),
        [(lines, LANES)],
        pltpu.with_memory_space_constraint(slab, pltpu.HBM),
        pltpu.with_memory_space_constraint(flips.reshape(outer, LANES), pltpu.HBM),
        specs=[HBM, HBM],
        out_specs=[HBM],
        scratch=[
            pltpu.VMEM((width, rows), jnp.float32),
            pltpu.VMEM((outer, LANES), jnp.int32),
            pltpu.VMEM((lines, LANES), jnp.float32),
            pltpu.VMEM((lines, LANES), jnp.float32),
            dma((width // 8,)),
            dma,
            dma((outer // A_LO,)),
        ],
        name="local_transform",
    )
    there = exchange(local, blocks)
    (hits,) = call(
        lambda *refs: hits_kernel(rows.bit_length() - 1, *refs),
        [(A_LO * blocks // LANES, LANES)],
        me,
        sampled.reshape(SAMPLES // LANES, LANES),
        specs=[SMEM, VMEM],
        name="sampled_hits",
    )
    there, hits = lax.optimization_barrier((there, hits))
    (whole,) = call(
        lambda *refs: blocks_kernel(blocks, *refs),
        [(lines, LANES)],
        there,
        out_specs=[HBM],
        scratch=[pltpu.VMEM((lines, LANES), jnp.float32)] * 2 + [dma((blocks // 64,))],
        name="block_transform",
    )
    back = exchange(whole, blocks)
    (partial,) = call(
        lambda *refs: gram_kernel(width, blocks, *refs),
        [(PACK, LANES)],
        whole,
        hits,
        scratch=[pltpu.VMEM((width * A_LO, blocks), jnp.float32)],
        name="gram_terms",
    )
    partial = sum_pairwise(partial, NEAR)
    one, two, three = from_others(partial, MIDDLE)
    partial = (partial + one) + (two + three)
    (partial,) = call(
        copies_kernel,
        [(1 << len(FAR), PACK, LANES)],
        partial,
        *from_others(partial, LAST),
        name="gram_copies",
    )
    back, partial = lax.optimization_barrier((back, partial))
    total = sum_over(partial, FAR)
    (mixed,) = call(
        lambda *refs: turn_kernel(width, *refs),
        [(width, rows)],
        back,
        out_specs=[HBM],
        scratch=[pltpu.VMEM((width, rows), jnp.float32), dma((outer // A_LO,))],
        name="turn_back",
    )
    gram, factor = call(
        factor_kernel,
        [(width, width)] * 2,
        total,
        scratch=[pltpu.VMEM((width, LANES), jnp.float32)],
        name="factor",
    )
    return (mixed, gram, factor)


def solution(mesh):
    placed = (P(None, AXES), P(AXES), P())
    return jax.shard_map(
        per_device,
        mesh=mesh,
        in_specs=placed,
        out_specs=(P(None, AXES), P(), P()),
        check_vma=False,
    )
```

```python
import math

import jax
import jax.numpy as jnp
from jax import lax
from jax.experimental import pallas as pl
from jax.experimental.pallas import tpu as pltpu
from jax.sharding import PartitionSpec as P

SAMPLES = 12288
AXES = ("group", "dev")
LANES = 128
A_LO = 16
PACK = 16
DENSE = 12
FAR = (5, 6, 7, 8)
NEAR = (0,)
MIDDLE = (1, 2)
LAST = (3, 4)
PIVOTS = 8
VMEM = pl.BlockSpec(memory_space=pltpu.VMEM)
HBM = pl.BlockSpec(memory_space=pltpu.HBM)
SMEM = pl.BlockSpec(memory_space=pltpu.SMEM)


def split3(x):
    hi = x.astype(jnp.bfloat16)
    rest = x - hi.astype(jnp.float32)
    mid = rest.astype(jnp.bfloat16)
    lo = (rest - mid.astype(jnp.float32)).astype(jnp.bfloat16)
    return hi, mid, lo


def dot_nt(x, y):
    return lax.dot_general(x, y, (((1,), (1,)), ((), ())), preferred_element_type=jnp.float32)


def local_kernel(scale, slab_ref, flips_ref, out_ref, field_ref, signs_ref, turned_ref, done_ref, in_sem, flip_sem, out_sem):
    width, rows = slab_ref.shape
    outer = rows // LANES
    flips_in = pltpu.make_async_copy(flips_ref, signs_ref, flip_sem)
    flips_in.start()
    slab_in = []
    for tile in range(width // 8):
        part = pl.ds(tile * 8, 8)
        slab_in.append(pltpu.make_async_copy(slab_ref.at[part], field_ref.at[part], in_sem.at[tile]))
        slab_in[-1].start()
    flips_in.wait()
    signs = (1 - 2 * signs_ref[...]).astype(jnp.float32) * scale
    for tile in range(width // 8):
        rows8 = pl.ds(tile * 8, 8)
        slab_in[tile].wait()
        for first in range(outer // 8):
            parts = []
            for k in range(8):
                a = k * (outer // 8) + first
                parts.append(field_ref[rows8, pl.ds(a * LANES, LANES)] * signs[a : a + 1, :])
            for half in (4, 2, 1):
                parts = butterfly(parts, half)
            for k in range(8):
                a = k * (outer // 8) + first
                field_ref[rows8, pl.ds(a * LANES, LANES)] = parts[k]
    per = width * A_LO // LANES
    out = []
    for a_hi in range(outer // A_LO):
        for first in range(a_hi * A_LO, (a_hi + 1) * A_LO, 8):
            for tile in range(width // 8):
                rows8 = pl.ds(tile * 8, 8)
                parts = [field_ref[rows8, pl.ds((first + k) * LANES, LANES)] for k in range(8)]
                for half in (4, 2, 1):
                    parts = butterfly(parts, half)
                for k in range(8):
                    field_ref[rows8, pl.ds((first + k) * LANES, LANES)] = parts[k]
        block = jnp.concatenate(
            [field_ref[:, pl.ds((a_hi * A_LO + a) * LANES, LANES)] for a in range(A_LO)], axis=0
        )
        for j in range(per):
            start = (a_hi * per + j) * LANES
            turned = block[j * LANES : (j + 1) * LANES, :].T
            parts = [turned[k : k + 8, :] for k in range(0, LANES, 8)]
            for half in (8, 4, 2, 1):
                parts = butterfly(parts, half)
            for k in range(LANES // 8):
                turned_ref[pl.ds(start + 8 * k, 8), :] = parts[k]
            parts = [turned_ref[pl.ds(start + k, LANES // 8, stride=8), :] for k in range(8)]
            for half in (4, 2, 1):
                parts = butterfly(parts, half)
            for k in range(8):
                done_ref[pl.ds((a_hi * LANES + k) * per + j, LANES // 8, stride=8 * per), :] = parts[k]
        part = pl.ds(a_hi * LANES * per, LANES * per)
        out.append(pltpu.make_async_copy(done_ref.at[part], out_ref.at[part], out_sem.at[a_hi]))
        out[-1].start()
    for copy in out:
        copy.wait()


def butterfly(parts, half):
    out = list(parts)
    for k in range(len(parts)):
        if not k & half:
            out[k] = parts[k] + parts[k | half]
            out[k | half] = parts[k] - parts[k | half]
    return out


def blocks_kernel(blocks, x_ref, out_ref, half_ref, y_ref, out_sem):
    per = x_ref.shape[0] // blocks
    far = blocks // 8
    for j in range(per):
        for first in range(0, far, 8):
            parts = [x_ref[pl.ds((k * far + first) * per + j, 8, stride=per), :] for k in range(8)]
            for half in (4, 2, 1):
                parts = butterfly(parts, half)
            for k in range(8):
                half_ref[pl.ds(j * blocks + k * far + first, 8), :] = parts[k]
    out = []
    for first in range(0, blocks, 64):
        for j in range(per):
            start = j * blocks + first
            parts = [half_ref[pl.ds(start + 8 * k, 8), :] for k in range(8)]
            for half in (4, 2, 1):
                parts = butterfly(parts, half)
            for k in range(8):
                half_ref[pl.ds(start + 8 * k, 8), :] = parts[k]
            parts = [half_ref[pl.ds(start + k, 8, stride=8), :] for k in range(8)]
            for half in (4, 2, 1):
                parts = butterfly(parts, half)
            for k in range(8):
                y_ref[pl.ds((first + k) * per + j, 8, stride=8 * per), :] = parts[k]
        part = pl.ds(first * per, 64 * per)
        out.append(pltpu.make_async_copy(y_ref.at[part], out_ref.at[part], out_sem.at[first // 64]))
        out[-1].start()
    for copy in out:
        copy.wait()


def gram_kernel(width, blocks, y_ref, hits_ref, packed_ref, turned_ref):
    per = y_ref.shape[0] // blocks
    for j in range(per):
        turned_ref[pl.ds(j * LANES, LANES), :] = y_ref[pl.ds(j, blocks, stride=per), :].T
    gram_terms(width, turned_ref, hits_ref, packed_ref)


def hits_kernel(local_bits, me_ref, sampled_ref, out_ref):
    me = me_ref[0]
    s = sampled_ref[...]
    low = s & ((1 << local_bits) - 1)
    block = s >> local_bits
    a = low >> 7
    owner = (a // A_LO) * LANES + (low & (LANES - 1))
    row = jnp.where(owner == me, (a & (A_LO - 1)) * 4 + (block >> 7), -1)
    col = block & (LANES - 1)
    total = jnp.zeros(out_ref.shape, jnp.float32)
    rows_iota = lax.broadcasted_iota(jnp.int32, out_ref.shape, 0)
    cols_iota = lax.broadcasted_iota(jnp.int32, (LANES, LANES), 0)
    for start in range(0, s.shape[0], 8):
        ones_r, ones_c = [], []
        for k in range(start, start + 8):
            ones_r.append(jnp.where(rows_iota == row[k : k + 1, :], 1.0, 0.0).astype(jnp.bfloat16))
            ones_c.append(jnp.where(cols_iota == col[k : k + 1, :], 1.0, 0.0).astype(jnp.bfloat16))
        total = total + dot_nt(jnp.concatenate(ones_r, axis=1), jnp.concatenate(ones_c, axis=1))
    out_ref[...] = total


def gram_terms(width, turned_ref, hits_ref, out_ref):
    blocks = turned_ref.shape[1]
    total = jnp.zeros((3 * width, 3 * width), jnp.float32)
    for a_lo in range(A_LO):
        stacked = []
        for k in range(blocks // LANES):
            picked = (
                turned_ref[pl.ds(a_lo * width, width), pl.ds(k * LANES, LANES)]
                * hits_ref[pl.ds(a_lo * 4 + k, 1), :]
            )
            stacked.append(jnp.concatenate(split3(picked), axis=0))
        stacked = jnp.concatenate(stacked, axis=1)
        total = total + dot_nt(stacked, stacked)
    gram = jnp.zeros((width, width), jnp.float32)
    for i, k in ((2, 0), (0, 2), (1, 1), (1, 0), (0, 1), (0, 0)):
        gram = gram + total[i * width : (i + 1) * width, k * width : (k + 1) * width]
    out_ref[...] = jnp.zeros_like(out_ref)
    at = 0
    for i in range(0, width, PACK):
        out_ref[:, pl.ds(at, width - i)] = gram[i : i + PACK, i:]
        at += width - i


def copies_kernel(x_ref, one_ref, two_ref, three_ref, out_ref, dense_ref):
    total = (x_ref[...] + one_ref[...]) + (two_ref[...] + three_ref[...])
    dense_ref[...] = total[:DENSE, :]
    for i in range(DENSE):
        row, at = DENSE + i // 3, i % 3 * 32
        dense_ref[pl.ds(i, 1), pl.ds(LANES - 32, 32)] = total[row : row + 1, at : at + 32]
    dense = dense_ref[...]
    for k in range(out_ref.shape[0] // DENSE):
        out_ref[pl.ds(k * DENSE, DENSE), :] = dense


def factor_kernel(x_ref, gram_ref, factor_ref, full_ref, packed_ref):
    width = gram_ref.shape[0]
    total = x_ref[pl.ds(0, DENSE), :]
    for k in range(1, x_ref.shape[0] // DENSE):
        total = total + x_ref[pl.ds(k * DENSE, DENSE), :]
    total = total / jnp.float32(SAMPLES)
    packed_ref[pl.ds(0, DENSE), :] = total
    for i in range(DENSE):
        packed_ref[pl.ds(DENSE + i // 3, 1), pl.ds(i % 3 * 32, 32)] = total[i : i + 1, LANES - 32 :]
    packed = packed_ref[...]
    full_ref[...] = jnp.zeros_like(full_ref)
    at = 0
    for i in range(0, width, PACK):
        full_ref[pl.ds(i, PACK), pl.ds(i, width - i)] = packed[:, at : at + width - i]
        at += width - i
    for i in range(0, width, PACK):
        for k in range(i + PACK, width, PACK):
            full_ref[pl.ds(k, PACK), pl.ds(i, PACK)] = full_ref[pl.ds(i, PACK), pl.ds(k, PACK)].T
    left = full_ref[...]
    gram_ref[...] = left[:, :width]
    lane = lax.broadcasted_iota(jnp.int32, (1, LANES), 1)
    upper = []
    for at in range(0, width, PIVOTS):
        rows = [left[at + i : at + i + 1, :] for i in range(PIVOTS)]
        cols = [jnp.broadcast_to(left[:, at + i : at + i + 1], left.shape) for i in range(PIVOTS)]
        pivot = [
            [jnp.broadcast_to(rows[i][:, at + k : at + k + 1], (1, LANES)) for k in range(PIVOTS)]
            for i in range(PIVOTS)
        ]
        for i in range(PIVOTS):
            inverse = 1.0 / pivot[i][i]
            for k in range(i + 1, PIVOTS):
                ratio = pivot[i][k] * inverse
                rows[k] = rows[k] - ratio * rows[i]
                cols[k] = cols[k] - ratio * cols[i]
                for m in range(k, PIVOTS):
                    pivot[k][m] = pivot[k][m] - ratio * pivot[i][m]
            upper.append(jnp.where(lane >= at + i, rows[i] / jnp.sqrt(pivot[i][i]), 0.0))
            left = left - cols[i] * (rows[i] * inverse)
    for i in range(width):
        factor_ref[pl.ds(i, 1), :] = upper[i][:, :width]


def turn_kernel(width, z_ref, out_ref, turned_ref, out_sem):
    per = width * A_LO // LANES
    out = []
    for a_hi in range(z_ref.shape[0] // (LANES * per)):
        turned = jnp.concatenate(
            [z_ref[pl.ds(a_hi * LANES * per + j, LANES, stride=per), :].T for j in range(per)], axis=0
        )
        for a_lo in range(A_LO):
            turned_ref[:, pl.ds((a_hi * A_LO + a_lo) * LANES, LANES)] = turned[a_lo * width : (a_lo + 1) * width, :]
        part = (slice(None), pl.ds(a_hi * A_LO * LANES, A_LO * LANES))
        out.append(pltpu.make_async_copy(turned_ref.at[part], out_ref.at[part], out_sem.at[a_hi]))
        out[-1].start()
    for copy in out:
        copy.wait()


def call(kernel, shapes, *operands, specs=None, out_specs=None, scratch=(), name=None):
    out = [jax.ShapeDtypeStruct(shape, jnp.float32) for shape in shapes]
    return pl.pallas_call(
        kernel,
        out_shape=out,
        in_specs=specs or [VMEM] * len(operands),
        out_specs=out_specs or [VMEM] * len(out),
        scratch_shapes=list(scratch),
        compiler_params=pltpu.CompilerParams(vmem_limit_bytes=48 * 1024 * 1024),
        name=name,
    )(*operands)


def exchange(x, blocks):
    shape = x.shape
    x = lax.all_to_all(x.reshape(blocks, x.size // blocks), AXES, 0, 0, tiled=True)
    return x.reshape(shape)


def from_all(x, bits):
    total = lax.axis_size(AXES)
    member = [sum((k >> n & 1) << bit for n, bit in enumerate(bits)) for k in range(1 << len(bits))]
    groups = [[i | m for m in member] for i in range(total) if not i & member[-1]]
    parts = x.reshape(len(member), x.size // len(member))
    return lax.all_to_all(parts, AXES, 0, 0, tiled=True, axis_index_groups=groups).reshape(x.shape)


def sum_pairwise(x, bits):
    for bit in bits:
        x = x + from_partner(x, 1 << bit)
    return x


def from_others(x, bits):
    return [from_partner(x, apart) for apart in (1 << bits[0], 1 << bits[1], 1 << bits[0] | 1 << bits[1])]


def from_partner(x, apart):
    return lax.ppermute(x, AXES, [(i, i ^ apart) for i in range(lax.axis_size(AXES))])


def per_device(slab, flips, sampled):
    width, rows = slab.shape
    blocks = lax.axis_size("group") * lax.axis_size("dev")
    scale = 1.0 / math.sqrt(rows * blocks)
    me = lax.axis_index(AXES).astype(jnp.int32).reshape(1)
    lines = width * rows // LANES
    outer = rows // LANES
    dma = pltpu.SemaphoreType.DMA

    (local,) = call(
        lambda *refs: local_kernel(scale, *refs),
        [(lines, LANES)],
        pltpu.with_memory_space_constraint(slab, pltpu.HBM),
        pltpu.with_memory_space_constraint(flips.reshape(outer, LANES), pltpu.HBM),
        specs=[HBM, HBM],
        out_specs=[HBM],
        scratch=[
            pltpu.VMEM((width, rows), jnp.float32),
            pltpu.VMEM((outer, LANES), jnp.int32),
            pltpu.VMEM((lines, LANES), jnp.float32),
            pltpu.VMEM((lines, LANES), jnp.float32),
            dma((width // 8,)),
            dma,
            dma((outer // A_LO,)),
        ],
        name="local_transform",
    )
    there = exchange(local, blocks)
    (hits,) = call(
        lambda *refs: hits_kernel(rows.bit_length() - 1, *refs),
        [(A_LO * blocks // LANES, LANES)],
        me,
        sampled.reshape(SAMPLES // LANES, LANES),
        specs=[SMEM, VMEM],
        name="sampled_hits",
    )
    there, hits = lax.optimization_barrier((there, hits))
    (whole,) = call(
        lambda *refs: blocks_kernel(blocks, *refs),
        [(lines, LANES)],
        there,
        out_specs=[HBM],
        scratch=[pltpu.VMEM((lines, LANES), jnp.float32)] * 2 + [dma((blocks // 64,))],
        name="block_transform",
    )
    back = exchange(whole, blocks)
    (partial,) = call(
        lambda *refs: gram_kernel(width, blocks, *refs),
        [(PACK, LANES)],
        whole,
        hits,
        scratch=[pltpu.VMEM((width * A_LO, blocks), jnp.float32)],
        name="gram_terms",
    )
    partial = sum_pairwise(partial, NEAR)
    one, two, three = from_others(partial, MIDDLE)
    partial = (partial + one) + (two + three)
    (partial,) = call(
        copies_kernel,
        [(DENSE << len(FAR), LANES)],
        partial,
        *from_others(partial, LAST),
        scratch=[pltpu.VMEM((DENSE, LANES), jnp.float32)],
        name="gram_copies",
    )
    back, partial = lax.optimization_barrier((back, partial))
    total = from_all(partial, FAR)
    (mixed,) = call(
        lambda *refs: turn_kernel(width, *refs),
        [(width, rows)],
        back,
        out_specs=[HBM],
        scratch=[pltpu.VMEM((width, rows), jnp.float32), dma((outer // A_LO,))],
        name="turn_back",
    )
    gram, factor = call(
        factor_kernel,
        [(width, width)] * 2,
        total,
        scratch=[pltpu.VMEM((width, LANES), jnp.float32), pltpu.VMEM((PACK, LANES), jnp.float32)],
        name="factor",
    )
    return (mixed, gram, factor)


def solution(mesh):
    placed = (P(None, AXES), P(AXES), P())
    return jax.shard_map(
        per_device,
        mesh=mesh,
        in_specs=placed,
        out_specs=(P(None, AXES), P(), P()),
        check_vma=False,
    )
```

```python
import math

import jax
import jax.numpy as jnp
from jax import lax
from jax.experimental import pallas as pl
from jax.experimental.pallas import tpu as pltpu
from jax.sharding import PartitionSpec as P

SAMPLES = 12288
AXES = ("group", "dev")
LANES = 128
A_LO = 16
PACK = 16
DENSE = 12
FAR = (5, 6, 7, 8)
NEAR = (0,)
MIDDLE = (1, 2)
LAST = (3, 4)
PIVOTS = 8
VMEM = pl.BlockSpec(memory_space=pltpu.VMEM)
HBM = pl.BlockSpec(memory_space=pltpu.HBM)
SMEM = pl.BlockSpec(memory_space=pltpu.SMEM)


def split3(x):
    hi = x.astype(jnp.bfloat16)
    rest = x - hi.astype(jnp.float32)
    mid = rest.astype(jnp.bfloat16)
    lo = (rest - mid.astype(jnp.float32)).astype(jnp.bfloat16)
    return hi, mid, lo


def dot_nt(x, y):
    return lax.dot_general(x, y, (((1,), (1,)), ((), ())), preferred_element_type=jnp.float32)


def local_kernel(scale, slab_ref, flips_ref, out_ref, field_ref, signs_ref, turned_ref, done_ref, in_sem, flip_sem, out_sem):
    width, rows = slab_ref.shape
    outer = rows // LANES
    flips_in = pltpu.make_async_copy(flips_ref, signs_ref, flip_sem)
    flips_in.start()
    slab_in = []
    for tile in range(width // 16):
        part = pl.ds(tile * 16, 16)
        slab_in.append(pltpu.make_async_copy(slab_ref.at[part], field_ref.at[part], in_sem.at[tile]))
        slab_in[-1].start()
    flips_in.wait()
    signs = (1 - 2 * signs_ref[...]).astype(jnp.float32) * scale
    for tile in range(width // 8):
        rows8 = pl.ds(tile * 8, 8)
        if tile % 2 == 0:
            slab_in[tile // 2].wait()
        for first in range(outer // 8):
            parts = []
            for k in range(8):
                a = k * (outer // 8) + first
                parts.append(field_ref[rows8, pl.ds(a * LANES, LANES)] * signs[a : a + 1, :])
            for half in (4, 2, 1):
                parts = butterfly(parts, half)
            for k in range(8):
                a = k * (outer // 8) + first
                field_ref[rows8, pl.ds(a * LANES, LANES)] = parts[k]
    per = width * A_LO // LANES
    out = []
    for a_hi in range(outer // A_LO):
        for first in range(a_hi * A_LO, (a_hi + 1) * A_LO, 8):
            for tile in range(width // 8):
                rows8 = pl.ds(tile * 8, 8)
                parts = [field_ref[rows8, pl.ds((first + k) * LANES, LANES)] for k in range(8)]
                for half in (4, 2, 1):
                    parts = butterfly(parts, half)
                for k in range(8):
                    field_ref[rows8, pl.ds((first + k) * LANES, LANES)] = parts[k]
        block = jnp.concatenate(
            [field_ref[:, pl.ds((a_hi * A_LO + a) * LANES, LANES)] for a in range(A_LO)], axis=0
        )
        for j in range(per):
            start = (a_hi * per + j) * LANES
            turned = block[j * LANES : (j + 1) * LANES, :].T
            parts = [turned[k : k + 8, :] for k in range(0, LANES, 8)]
            for half in (8, 4, 2, 1):
                parts = butterfly(parts, half)
            for k in range(LANES // 8):
                turned_ref[pl.ds(start + 8 * k, 8), :] = parts[k]
            parts = [turned_ref[pl.ds(start + k, LANES // 8, stride=8), :] for k in range(8)]
            for half in (4, 2, 1):
                parts = butterfly(parts, half)
            for k in range(8):
                done_ref[pl.ds((a_hi * LANES + k) * per + j, LANES // 8, stride=8 * per), :] = parts[k]
        part = pl.ds(a_hi * LANES * per, LANES * per)
        out.append(pltpu.make_async_copy(done_ref.at[part], out_ref.at[part], out_sem.at[a_hi]))
        out[-1].start()
    for copy in out:
        copy.wait()


def butterfly(parts, half):
    out = list(parts)
    for k in range(len(parts)):
        if not k & half:
            out[k] = parts[k] + parts[k | half]
            out[k | half] = parts[k] - parts[k | half]
    return out


def blocks_kernel(blocks, x_ref, out_ref, half_ref, y_ref, out_sem):
    per = x_ref.shape[0] // blocks
    far = blocks // 8
    for j in range(per):
        for first in range(0, far, 8):
            parts = [x_ref[pl.ds((k * far + first) * per + j, 8, stride=per), :] for k in range(8)]
            for half in (4, 2, 1):
                parts = butterfly(parts, half)
            for k in range(8):
                half_ref[pl.ds(j * blocks + k * far + first, 8), :] = parts[k]
    out = []
    for first in range(0, blocks, 64):
        for j in range(per):
            start = j * blocks + first
            parts = [half_ref[pl.ds(start + 8 * k, 8), :] for k in range(8)]
            for half in (4, 2, 1):
                parts = butterfly(parts, half)
            for k in range(8):
                half_ref[pl.ds(start + 8 * k, 8), :] = parts[k]
            parts = [half_ref[pl.ds(start + k, 8, stride=8), :] for k in range(8)]
            for half in (4, 2, 1):
                parts = butterfly(parts, half)
            for k in range(8):
                y_ref[pl.ds((first + k) * per + j, 8, stride=8 * per), :] = parts[k]
        part = pl.ds(first * per, 64 * per)
        out.append(pltpu.make_async_copy(y_ref.at[part], out_ref.at[part], out_sem.at[first // 64]))
        out[-1].start()
    for copy in out:
        copy.wait()


def gram_kernel(width, blocks, y_ref, hits_ref, packed_ref, turned_ref):
    per = y_ref.shape[0] // blocks
    for j in range(per):
        turned_ref[pl.ds(j * LANES, LANES), :] = y_ref[pl.ds(j, blocks, stride=per), :].T
    gram_terms(width, turned_ref, hits_ref, packed_ref)


def hits_kernel(local_bits, me_ref, sampled_ref, out_ref):
    me = me_ref[0]
    s = sampled_ref[...]
    low = s & ((1 << local_bits) - 1)
    block = s >> local_bits
    a = low >> 7
    owner = (a // A_LO) * LANES + (low & (LANES - 1))
    row = jnp.where(owner == me, (a & (A_LO - 1)) * 4 + (block >> 7), -1)
    col = block & (LANES - 1)
    total = jnp.zeros(out_ref.shape, jnp.float32)
    rows_iota = lax.broadcasted_iota(jnp.int32, out_ref.shape, 0)
    cols_iota = lax.broadcasted_iota(jnp.int32, (LANES, LANES), 0)
    for start in range(0, s.shape[0], 8):
        ones_r, ones_c = [], []
        for k in range(start, start + 8):
            ones_r.append(jnp.where(rows_iota == row[k : k + 1, :], 1.0, 0.0).astype(jnp.bfloat16))
            ones_c.append(jnp.where(cols_iota == col[k : k + 1, :], 1.0, 0.0).astype(jnp.bfloat16))
        total = total + dot_nt(jnp.concatenate(ones_r, axis=1), jnp.concatenate(ones_c, axis=1))
    out_ref[...] = total


def gram_terms(width, turned_ref, hits_ref, out_ref):
    blocks = turned_ref.shape[1]
    total = jnp.zeros((3 * width, 3 * width), jnp.float32)
    for a_lo in range(A_LO):
        stacked = []
        for k in range(blocks // LANES):
            picked = (
                turned_ref[pl.ds(a_lo * width, width), pl.ds(k * LANES, LANES)]
                * hits_ref[pl.ds(a_lo * 4 + k, 1), :]
            )
            stacked.append(jnp.concatenate(split3(picked), axis=0))
        stacked = jnp.concatenate(stacked, axis=1)
        total = total + dot_nt(stacked, stacked)
    gram = jnp.zeros((width, width), jnp.float32)
    for i, k in ((2, 0), (0, 2), (1, 1), (1, 0), (0, 1), (0, 0)):
        gram = gram + total[i * width : (i + 1) * width, k * width : (k + 1) * width]
    out_ref[...] = jnp.zeros_like(out_ref)
    at = 0
    for i in range(0, width, PACK):
        out_ref[:, pl.ds(at, width - i)] = gram[i : i + PACK, i:]
        at += width - i


def copies_kernel(x_ref, one_ref, two_ref, three_ref, out_ref, dense_ref):
    total = (x_ref[...] + one_ref[...]) + (two_ref[...] + three_ref[...])
    dense_ref[...] = total[:DENSE, :]
    for i in range(DENSE):
        row, at = DENSE + i // 3, i % 3 * 32
        dense_ref[pl.ds(i, 1), pl.ds(LANES - 32, 32)] = total[row : row + 1, at : at + 32]
    dense = dense_ref[...]
    for k in range(out_ref.shape[0] // DENSE):
        out_ref[pl.ds(k * DENSE, DENSE), :] = dense


def factor_kernel(x_ref, gram_ref, factor_ref, full_ref, packed_ref):
    width = gram_ref.shape[0]
    total = x_ref[pl.ds(0, DENSE), :]
    for k in range(1, x_ref.shape[0] // DENSE):
        total = total + x_ref[pl.ds(k * DENSE, DENSE), :]
    total = total / jnp.float32(SAMPLES)
    packed_ref[pl.ds(0, DENSE), :] = total
    for i in range(DENSE):
        packed_ref[pl.ds(DENSE + i // 3, 1), pl.ds(i % 3 * 32, 32)] = total[i : i + 1, LANES - 32 :]
    packed = packed_ref[...]
    full_ref[...] = jnp.zeros_like(full_ref)
    at = 0
    for i in range(0, width, PACK):
        full_ref[pl.ds(i, PACK), pl.ds(i, width - i)] = packed[:, at : at + width - i]
        at += width - i
    for i in range(0, width, PACK):
        for k in range(i + PACK, width, PACK):
            full_ref[pl.ds(k, PACK), pl.ds(i, PACK)] = full_ref[pl.ds(i, PACK), pl.ds(k, PACK)].T
    left = full_ref[...]
    gram_ref[...] = left[:, :width]
    lane = lax.broadcasted_iota(jnp.int32, (1, LANES), 1)
    upper = []
    for at in range(0, width, PIVOTS):
        rows = [left[at + i : at + i + 1, :] for i in range(PIVOTS)]
        cols = [jnp.broadcast_to(left[:, at + i : at + i + 1], left.shape) for i in range(PIVOTS)]
        pivot = [
            [jnp.broadcast_to(rows[i][:, at + k : at + k + 1], (1, LANES)) for k in range(PIVOTS)]
            for i in range(PIVOTS)
        ]
        for i in range(PIVOTS):
            inverse = 1.0 / pivot[i][i]
            for k in range(i + 1, PIVOTS):
                ratio = pivot[i][k] * inverse
                rows[k] = rows[k] - ratio * rows[i]
                cols[k] = cols[k] - ratio * cols[i]
                for m in range(k, PIVOTS):
                    pivot[k][m] = pivot[k][m] - ratio * pivot[i][m]
            upper.append(jnp.where(lane >= at + i, rows[i] / jnp.sqrt(pivot[i][i]), 0.0))
            left = left - cols[i] * (rows[i] * inverse)
    for i in range(width):
        factor_ref[pl.ds(i, 1), :] = upper[i][:, :width]


def turn_kernel(width, z_ref, out_ref, turned_ref, out_sem):
    per = width * A_LO // LANES
    out = []
    for a_hi in range(z_ref.shape[0] // (LANES * per)):
        turned = jnp.concatenate(
            [z_ref[pl.ds(a_hi * LANES * per + j, LANES, stride=per), :].T for j in range(per)], axis=0
        )
        for a_lo in range(A_LO):
            turned_ref[:, pl.ds((a_hi * A_LO + a_lo) * LANES, LANES)] = turned[a_lo * width : (a_lo + 1) * width, :]
        part = (slice(None), pl.ds(a_hi * A_LO * LANES, A_LO * LANES))
        out.append(pltpu.make_async_copy(turned_ref.at[part], out_ref.at[part], out_sem.at[a_hi]))
        out[-1].start()
    for copy in out:
        copy.wait()


def call(kernel, shapes, *operands, specs=None, out_specs=None, scratch=(), name=None):
    out = [jax.ShapeDtypeStruct(shape, jnp.float32) for shape in shapes]
    return pl.pallas_call(
        kernel,
        out_shape=out,
        in_specs=specs or [VMEM] * len(operands),
        out_specs=out_specs or [VMEM] * len(out),
        scratch_shapes=list(scratch),
        compiler_params=pltpu.CompilerParams(vmem_limit_bytes=48 * 1024 * 1024),
        name=name,
    )(*operands)


def exchange(x, blocks):
    shape = x.shape
    x = lax.all_to_all(x.reshape(blocks, x.size // blocks), AXES, 0, 0, tiled=True)
    return x.reshape(shape)


def from_all(x, bits):
    total = lax.axis_size(AXES)
    member = [sum((k >> n & 1) << bit for n, bit in enumerate(bits)) for k in range(1 << len(bits))]
    groups = [[i | m for m in member] for i in range(total) if not i & member[-1]]
    parts = x.reshape(len(member), x.size // len(member))
    return lax.all_to_all(parts, AXES, 0, 0, tiled=True, axis_index_groups=groups).reshape(x.shape)


def sum_pairwise(x, bits):
    for bit in bits:
        x = x + from_partner(x, 1 << bit)
    return x


def from_others(x, bits):
    return [from_partner(x, apart) for apart in (1 << bits[0], 1 << bits[1], 1 << bits[0] | 1 << bits[1])]


def from_partner(x, apart):
    return lax.ppermute(x, AXES, [(i, i ^ apart) for i in range(lax.axis_size(AXES))])


def per_device(slab, flips, sampled):
    width, rows = slab.shape
    blocks = lax.axis_size("group") * lax.axis_size("dev")
    scale = 1.0 / math.sqrt(rows * blocks)
    me = lax.axis_index(AXES).astype(jnp.int32).reshape(1)
    lines = width * rows // LANES
    outer = rows // LANES
    dma = pltpu.SemaphoreType.DMA

    (local,) = call(
        lambda *refs: local_kernel(scale, *refs),
        [(lines, LANES)],
        pltpu.with_memory_space_constraint(slab, pltpu.HBM),
        pltpu.with_memory_space_constraint(flips.reshape(outer, LANES), pltpu.HBM),
        specs=[HBM, HBM],
        out_specs=[HBM],
        scratch=[
            pltpu.VMEM((width, rows), jnp.float32),
            pltpu.VMEM((outer, LANES), jnp.int32),
            pltpu.VMEM((lines, LANES), jnp.float32),
            pltpu.VMEM((lines, LANES), jnp.float32),
            dma((width // 16,)),
            dma,
            dma((outer // A_LO,)),
        ],
        name="local_transform",
    )
    there = exchange(local, blocks)
    (hits,) = call(
        lambda *refs: hits_kernel(rows.bit_length() - 1, *refs),
        [(A_LO * blocks // LANES, LANES)],
        me,
        sampled.reshape(SAMPLES // LANES, LANES),
        specs=[SMEM, VMEM],
        name="sampled_hits",
    )
    there, hits = lax.optimization_barrier((there, hits))
    (whole,) = call(
        lambda *refs: blocks_kernel(blocks, *refs),
        [(lines, LANES)],
        there,
        out_specs=[HBM],
        scratch=[pltpu.VMEM((lines, LANES), jnp.float32)] * 2 + [dma((blocks // 64,))],
        name="block_transform",
    )
    back = exchange(whole, blocks)
    (partial,) = call(
        lambda *refs: gram_kernel(width, blocks, *refs),
        [(PACK, LANES)],
        whole,
        hits,
        scratch=[pltpu.VMEM((width * A_LO, blocks), jnp.float32)],
        name="gram_terms",
    )
    partial = sum_pairwise(partial, NEAR)
    one, two, three = from_others(partial, MIDDLE)
    partial = (partial + one) + (two + three)
    (partial,) = call(
        copies_kernel,
        [(DENSE << len(FAR), LANES)],
        partial,
        *from_others(partial, LAST),
        scratch=[pltpu.VMEM((DENSE, LANES), jnp.float32)],
        name="gram_copies",
    )
    back, partial = lax.optimization_barrier((back, partial))
    total = from_all(partial, FAR)
    (mixed,) = call(
        lambda *refs: turn_kernel(width, *refs),
        [(width, rows)],
        back,
        out_specs=[HBM],
        scratch=[pltpu.VMEM((width, rows), jnp.float32), dma((outer // A_LO,))],
        name="turn_back",
    )
    gram, factor = call(
        factor_kernel,
        [(width, width)] * 2,
        total,
        scratch=[pltpu.VMEM((width, LANES), jnp.float32), pltpu.VMEM((PACK, LANES), jnp.float32)],
        name="factor",
    )
    return (mixed, gram, factor)


def solution(mesh):
    placed = (P(None, AXES), P(AXES), P())
    return jax.shard_map(
        per_device,
        mesh=mesh,
        in_specs=placed,
        out_specs=(P(None, AXES), P(), P()),
        check_vma=False,
    )
```
